512 devices in a mesh: src: 16 (over z), tgt: 32 (over y, x, core).
Axes of the slice: x: 4, y: 4, z: 16, core: 2. Of those that a mesh axis runs over, the one named last changes fastest.
Arguments:
- source_latents: float32 [32768, 64], P(('src', 'tgt')), may hold values from -20 to 20
- target_latents: float32 [32768, 64], P('tgt'), may hold values from -20 to 20
Outputs:
- source_potential: float32 [32768], P('src')
- target_potential: float32 [32768], P('tgt')
- row_mass: float32 [32768], P('src')
The draws below stay inside these ranges and needn't reach their ends.
All inputs are finite; a program needn't handle non-finite values.
Results may differ from the reference program's by a relative error of at most 0.00035.
Values sent between devices are 32-bit elements; how exact they have to be, the bound alone decides.
A program may use at most 64 MiB of HBM per device.

```python
import math
import jax
import jax.numpy as jnp
from jax import lax

D = 64
ITERS = 4
N = 32768
M = 32768


def draw_source_latents(key, part):
    key = jax.random.fold_in(key, 11)
    first = jax.random.fold_in(key, 0)
    third = jax.random.fold_in(key, 2)
    place = jnp.arange(N, dtype=jnp.float32) / N
    distant = (jnp.arange(N) % 4096 == 7).astype(jnp.float32)[:, None]
    values = jax.random.normal(first, (N, D), jnp.float32) * (0.8 + 0.6 * place)[:, None]
    shift = jax.random.uniform(third, (N, 1), jnp.float32, 12.0, 14.0)
    return values * (1.0 - 0.8 * distant) + distant * shift


def draw_target_latents(key, part):
    key = jax.random.fold_in(key, 23)
    first = jax.random.fold_in(key, 0)
    third = jax.random.fold_in(key, 2)
    place = jnp.arange(M, dtype=jnp.float32) / M
    distant = (jnp.arange(M) % 4096 == 131).astype(jnp.float32)[:, None]
    values = jax.random.normal(first, (M, D), jnp.float32) * (0.8 + 0.6 * place)[:, None]
    shift = jax.random.uniform(third, (M, 1), jnp.float32, 12.0, 14.0)
    return values * (1.0 - 0.8 * distant) - distant * shift


def setup_inputs(seed: int = 0) -> dict:
    splits = jax.random.split(jax.random.key(seed), 3)
    return {
        "source_latents": draw_source_latents(jax.random.fold_in(splits[2], 71), 0),
        "target_latents": draw_target_latents(jax.random.fold_in(splits[2], 71), 0),
    }


def reference(source_latents, target_latents):
    n_source, width = source_latents.shape
    n_target = target_latents.shape[0]
    src_square = jnp.sum(source_latents * source_latents)
    tgt_square = jnp.sum(target_latents * target_latents)
    src_center = jnp.sum(source_latents, 0) / n_source
    tgt_center = jnp.sum(target_latents, 0) / n_target
    mean_cost = src_square / n_source + tgt_square / n_target - 2.0 * jnp.sum(src_center * tgt_center)
    regular = 0.05 * mean_cost
    block = math.gcd(n_source, 1024)
    blocks = source_latents.reshape(n_source // block, block, width)
    tgt_norms = jnp.sum(target_latents * target_latents, 1)

    def scaled_block(piece):
        src_norms = jnp.sum(piece * piece, 1)
        cross = lax.dot_general(piece, target_latents, (((1,), (1,)), ((), ())), precision=lax.Precision.HIGHEST, preferred_element_type=jnp.float32)
        return (src_norms[:, None] + tgt_norms[None, :] - 2.0 * cross) / regular

    def row_lse(potential_v):
        def one_block(piece):
            return jax.nn.logsumexp(potential_v[None, :] - scaled_block(piece), axis=1)
        return lax.map(one_block, blocks).reshape(n_source)

    def col_lse(potential_u):
        pieces_u = potential_u.reshape(n_source // block, block)

        def advance(carry, item):
            piece, part_u = item
            scores = part_u[:, None] - scaled_block(piece)
            top = jnp.max(scores, 0)
            best = jnp.maximum(carry[0], top)
            total = carry[1] * jnp.exp(carry[0] - best) + jnp.sum(jnp.exp(scores - top[None, :]), 0) * jnp.exp(top - best)
            return (best, total), None

        start = (jnp.full((n_target,), -jnp.inf, jnp.float32), jnp.zeros((n_target,), jnp.float32))
        final, unused = lax.scan(advance, start, (blocks, pieces_u))
        return final[0] + jnp.log(final[1])

    log_source = -math.log(n_source)
    log_target = -math.log(n_target)
    potential_v = jnp.zeros((n_target,), jnp.float32)
    potential_u = jnp.zeros((n_source,), jnp.float32)
    for step in range(ITERS):
        potential_u = log_source - row_lse(potential_v)
        potential_v = log_target - col_lse(potential_u)
    updated = log_source - row_lse(potential_v)
    row_mass = jnp.exp(potential_u - updated)
    return potential_u, potential_v, row_mass
```

```python
import functools
import math

import jax
import jax.numpy as jnp
from jax import lax
from jax.experimental import pallas as pl
from jax.experimental.pallas import tpu as pltpu
from jax.sharding import PartitionSpec as P

ITERS = 4
EDGE = 4
CHIPS = EDGE * EDGE
LAYERS = 16
WIDTH = 64
ROWS = 2048
COLS = 1024
ROW_TILES = ROWS // 128
COL_TILES = COLS // 128
DEPTH = 8 * WIDTH
CELLS = 32768
LOG_CELLS = math.log2(CELLS)
LIFT = 30.0
SCALE = 90.0
MESH = pl.DeviceIdType.MESH


def hops(step):
    return min(step, EDGE - step)


PLANE = sorted(
    ((dy, dx) for dy in range(EDGE) for dx in range(EDGE) if dy or dx),
    key=lambda step: -hops(step[0]) - hops(step[1]),
)
RING = sorted(range(1, LAYERS), key=lambda step: -min(step, LAYERS - step))


def split3(value):
    high = value.astype(jnp.bfloat16)
    rest = value - high.astype(jnp.float32)
    mid = rest.astype(jnp.bfloat16)
    low = (rest - mid.astype(jnp.float32)).astype(jnp.bfloat16)
    return high, mid, low


def kernel(
    x_hbm, yt_hbm, u_out, v_out, mass_out,
    x_in, x_pad, yt, ya, xt, tile, gx,
    stat_send, stat_slots, zstat_send, zstat_slots,
    row_send, row_sib, row_slots, col_send, col_slots,
    col_part, col_wide, row_max, row_norm, row_base, col_base, col_gain, alpha,
    in_sem, stat_sems, zstat_sems, gx_sems, fwd_sems,
    row_send_sem, row_sems, sib_send_sem, sib_sems, col_send_sem, col_sems,
):
    layer = lax.axis_index("src")
    place = lax.axis_index("tgt")
    core = lax.rem(place, 2)
    chip = place // 2
    px = lax.rem(chip, EDGE)
    py = chip // EDGE
    sibling = (layer, chip * 2 + 1 - core)

    def plane_chip(step):
        return lax.rem(py + step[0], EDGE) * EDGE + lax.rem(px + step[1], EDGE)

    plane_same = [(layer, plane_chip(step) * 2 + core) for step in PLANE]
    plane_other = [(layer, plane_chip(step) * 2 + 1 - core) for step in PLANE]
    ring = [(lax.rem(layer + step, LAYERS), place) for step in RING]

    def wait_bytes(ref, sem):
        pltpu.make_async_copy(ref, ref, sem).wait()

    def push(src, dst, send_sem, recv_sem, peer):
        pltpu.make_async_remote_copy(
            src_ref=src, dst_ref=dst, send_sem=send_sem, recv_sem=recv_sem,
            device_id=peer, device_id_type=MESH,
        ).start()

    x_pad[...] = jnp.zeros_like(x_pad)
    x_copy = pltpu.make_async_copy(x_hbm, x_in, in_sem.at[0])
    y_copy = pltpu.make_async_copy(yt_hbm, yt, in_sem.at[1])
    x_copy.start()
    y_copy.start()
    barrier = pltpu.get_barrier_semaphore()
    peers = ring + plane_same + plane_other + [sibling]
    for peer in peers:
        pl.semaphore_signal(barrier, inc=1, device_id=peer, device_id_type=MESH)
    x_copy.wait()
    y_copy.wait()
    x_pad[0:WIDTH, 0:WIDTH] = x_in[...]

    lanes = lax.broadcasted_iota(jnp.int32, (1, 128), 1)
    left = lanes < WIDTH

    x_wide = x_pad[...]
    x_turned = x_wide.T
    packed = x_turned[0:32, :] + pltpu.roll(x_turned[32:64, :], 64, 1)
    gx[core, chip] = packed

    y_sum = jnp.zeros((1, 128), jnp.float32)
    y_square = jnp.zeros((1, 128), jnp.float32)
    for block in range(COL_TILES):
        at = slice(block * 128, block * 128 + 128)
        piece = yt[:, at]
        wide = jnp.concatenate([piece, piece], 0).T
        square = wide * wide
        y_sum += jnp.sum(wide, 0, keepdims=True)
        y_square += jnp.sum(square, 0, keepdims=True)
        norm = jnp.sum(jnp.where(left, square, 0.0), 1, keepdims=True)
        high, mid, low = split3(wide)
        ya[at, 0:128] = high
        ya[at, 128:256] = mid
        ya[at, 256:384] = jnp.where(left, low.astype(jnp.float32), high.astype(jnp.float32)).astype(jnp.bfloat16)
        nh, nm, nl = split3(jnp.broadcast_to(norm, (128, 128)))
        tail = jnp.where(lanes == 0, nh.astype(jnp.float32), jnp.where(lanes == 1, nm.astype(jnp.float32), nl.astype(jnp.float32)))
        ya[at, 384:512] = jnp.where(lanes < 3, tail, 0.0).astype(jnp.bfloat16)
    x_sum = jnp.sum(x_wide, 0, keepdims=True)
    x_square = jnp.sum(x_wide * x_wide, 0, keepdims=True)
    stat_send[0:1, :] = jnp.where(left, x_sum, y_sum)
    stat_send[1:2, :] = jnp.where(left, x_square, y_square)
    stat_slots[place] = stat_send[...]

    pl.semaphore_wait(barrier, len(peers))

    for peer in plane_same + plane_other + [sibling]:
        push(stat_send, stat_slots.at[place], stat_sems.at[0], stat_sems.at[1], peer)
    for peer in plane_same:
        push(gx.at[core, chip], gx.at[core, chip], gx_sems.at[0], gx_sems.at[1], peer)
    wait_bytes(stat_slots.at[0 : 2 * CHIPS - 1], stat_sems.at[1])
    zstat_send[...] = jnp.sum(stat_slots[...], 0)
    zstat_slots[layer] = zstat_send[...]
    for peer in ring:
        push(zstat_send, zstat_slots.at[layer], zstat_sems.at[0], zstat_sems.at[1], peer)
    wait_bytes(gx.at[0, 0 : CHIPS - 1], gx_sems.at[1])
    push(gx.at[core], gx.at[core], fwd_sems.at[0], fwd_sems.at[1], sibling)
    wait_bytes(gx.at[0], fwd_sems.at[1])

    tail_row = lax.broadcasted_iota(jnp.int32, (128, 256), 0)
    tail_x = jnp.where(tail_row < 3, -1.0, 0.0).astype(jnp.bfloat16)

    def multiply(q, carry):
        halves = []
        for k in range(2):
            one = gx[0, 2 * q + k]
            two = gx[1, 2 * q + k]
            top = jnp.where(left, one, pltpu.roll(two, 64, 1))
            low = jnp.where(left, pltpu.roll(one, 64, 1), two)
            halves.append(jnp.concatenate([top, low], 0))
        full = jnp.concatenate(halves, 1)
        norm = jnp.sum(full * full, 0, keepdims=True)
        high, mid, low = split3(full * 2.0)
        xt[0:64, :] = high
        xt[64:128, :] = mid
        xt[128:192, :] = high
        xt[192:256, :] = mid
        xt[256:320, :] = high
        xt[320:384, :] = low
        xt[384:512, :] = tail_x
        product = jnp.dot(ya[...], xt[...], preferred_element_type=jnp.float32)
        at = pl.ds(pl.multiple_of(q * 256, 256), 256)
        tile[:, at] = product
        top = jnp.max(product, 0, keepdims=True)
        for k in range(2):
            row_max[pl.ds(2 * q + k, 1), :] = top[:, k * 128 : k * 128 + 128]
            row_norm[pl.ds(2 * q + k, 1), :] = norm[:, k * 128 : k * 128 + 128]
        return carry

    lax.fori_loop(0, ROWS // 256, multiply, 0)

    wait_bytes(zstat_slots.at[0 : LAYERS - 1], zstat_sems.at[1])
    total = jnp.sum(zstat_slots[...], 0) * jnp.where(left, 1.0 / CELLS, 1.0 / (CELLS * LAYERS))
    means = total[0:1, :]
    mean_cost = jnp.sum(total[1:2, :] - means * pltpu.roll(means, 64, 1), 1, keepdims=True)
    kappa = jnp.broadcast_to(math.log2(math.e) / (0.05 * mean_cost), (8, 128))

    def lane(t):
        return slice(t * 128, t * 128 + 128)

    def spread(ref, t):
        return jnp.broadcast_to(ref[t : t + 1, :], (8, 128))

    def row_exchange(parity, join):
        push(row_send, row_sib.at[parity], sib_send_sem, sib_sems.at[parity], sibling)
        wait_bytes(row_sib.at[parity], sib_sems.at[parity])
        wait_bytes(row_send, sib_send_sem)
        both = join(row_send[...], row_sib[parity])
        row_send[...] = both
        row_slots[parity, chip] = both
        for peer in plane_same:
            push(row_send, row_slots.at[parity, chip], row_send_sem, row_sems.at[parity], peer)
        wait_bytes(row_slots.at[parity, 0 : CHIPS - 1], row_sems.at[parity])
        wait_bytes(row_slots.at[parity, 0 : CHIPS - 1], row_send_sem)

    def col_exchange(parity):
        col_slots[parity, layer] = col_send[...]
        for peer in ring:
            push(col_send, col_slots.at[parity, layer], col_send_sem, col_sems.at[parity], peer)
        wait_bytes(col_slots.at[parity, 0 : LAYERS - 1], col_sems.at[parity])
        wait_bytes(col_slots.at[parity, 0 : LAYERS - 1], col_send_sem)

    def lse_pair(a, b):
        top = jnp.maximum(a, b)
        return top + jnp.log2(jnp.exp2(a - top) + jnp.exp2(b - top))

    def lse_slots(slots):
        top = jnp.max(slots, 0)
        return top + jnp.log2(jnp.sum(jnp.exp2(slots - top[None]), 0))

    def col_lanes(ref, pick):
        for block in range(COL_TILES):
            col_send[block : block + 1, :] = pick(ref[block * 128 : block * 128 + 128, :].T)

    def add_sublanes(block):
        return jnp.sum(block, 0, keepdims=True)

    row_max[...] = row_max[...] * kappa[0:1, :]
    GROUP = 4

    def first_rows(g, accs):
        accs = list(accs)
        for k in range(GROUP):
            at = pl.ds(pl.multiple_of(g * 8 * GROUP, 8) + 8 * k, 8)
            for t in range(ROW_TILES):
                accs[t] += jnp.exp2(tile[at, lane(t)] * kappa - spread(row_max, t))
        return tuple(accs)

    zeros = tuple(jnp.zeros((8, 128), jnp.float32) for _ in range(ROW_TILES))
    accs = lax.fori_loop(0, COLS // (8 * GROUP), first_rows, zeros)
    for t in range(ROW_TILES):
        row_send[t : t + 1, :] = row_max[t : t + 1, :] + jnp.log2(jnp.sum(accs[t], 0, keepdims=True))
    row_exchange(0, lse_pair)
    row_base[...] = -LOG_CELLS - lse_slots(row_slots[0])

    def first_max(g, carry):
        for k in range(GROUP):
            at = pl.ds(pl.multiple_of(g * 8 * GROUP, 8) + 8 * k, 8)
            top = tile[at, lane(0)] * kappa + spread(row_base, 0)
            for t in range(1, ROW_TILES):
                top = jnp.maximum(top, tile[at, lane(t)] * kappa + spread(row_base, t))
            col_part[at, :] = top
        return carry

    lax.fori_loop(0, COLS // (8 * GROUP), first_max, 0)
    for block in range(COL_TILES):
        at = slice(block * 128, block * 128 + 128)
        col_wide[at, :] = jnp.broadcast_to(jnp.max(col_part[at, :], 1, keepdims=True) - LIFT, (128, 128))

    def first_cols(g, carry):
        for k in range(GROUP):
            at = pl.ds(pl.multiple_of(g * 8 * GROUP, 8) + 8 * k, 8)
            top = col_wide[at, :]
            acc = None
            for t in range(ROW_TILES):
                power = jnp.exp2((tile[at, lane(t)] * kappa + spread(row_base, t)) - top)
                tile[at, lane(t)] = power
                acc = power if acc is None else acc + power
            col_part[at, :] = acc
        return carry

    lax.fori_loop(0, COLS // (8 * GROUP), first_cols, 0)
    col_lanes(col_wide, lambda block: block[0:1, :])
    col_gain[...] = col_send[...]
    col_lanes(col_part, add_sublanes)
    col_send[...] = col_gain[...] + jnp.log2(col_send[...])
    col_exchange(0)
    col_base[...] = -LOG_CELLS - lse_slots(col_slots[0])
    col_gain[...] = jnp.exp2(col_gain[...] + col_base[...] + SCALE)

    def spread_cols(value):
        turned = value.T
        for block in range(COL_TILES):
            col_wide[block * 128 : block * 128 + 128, :] = jnp.broadcast_to(turned[:, block : block + 1], (128, 128))

    def row_step(parity):
        def add_rows(g, accs):
            accs = list(accs)
            for k in range(GROUP):
                at = pl.ds(pl.multiple_of(g * 8 * GROUP, 8) + 8 * k, 8)
                gain = col_wide[at, :]
                for t in range(ROW_TILES):
                    accs[t] += tile[at, lane(t)] * gain
            return tuple(accs)

        accs = lax.fori_loop(0, COLS // (8 * GROUP), add_rows, zeros)
        for t in range(ROW_TILES):
            row_send[t : t + 1, :] = jnp.sum(accs[t], 0, keepdims=True)
        row_exchange(parity, jnp.add)
        return jnp.sum(row_slots[parity], 0)

    def col_step(parity):
        def add_cols(g, carry):
            for k in range(GROUP):
                at = pl.ds(pl.multiple_of(g * 8 * GROUP, 8) + 8 * k, 8)
                parts = [tile[at, lane(t)] * spread(alpha, t) for t in range(ROW_TILES)]
                while len(parts) > 1:
                    parts = [parts[i] + parts[i + 1] for i in range(0, len(parts), 2)]
                col_part[at, :] = parts[0]
            return carry

        lax.fori_loop(0, COLS // (8 * GROUP), add_cols, 0)
        col_lanes(col_part, add_sublanes)
        col_send[...] = col_send[...] * col_gain[...]
        col_exchange(parity)
        return jnp.sum(col_slots[parity], 0)

    ratio = 2.0 ** (SCALE - LOG_CELLS)
    spread_cols(col_gain[...])

    def iterate(step, carry):
        parity = lax.rem(step, 2)
        alpha[...] = ratio / row_step(parity)
        beta = ratio / col_step(parity)
        v_out[...] = (col_base[...] + jnp.log2(beta)) * math.log(2.0)
        spread_cols(beta * col_gain[...])
        return carry

    lax.fori_loop(1, ITERS, iterate, 0)
    u_out[...] = (row_base[...] + row_norm[...] * kappa[0:1, :] + jnp.log2(alpha[...])) * math.log(2.0)
    mass_out[...] = alpha[...] * (row_step(ITERS % 2) * (1.0 / ratio))
    wait_bytes(stat_slots.at[0 : 2 * CHIPS - 1], stat_sems.at[0])
    wait_bytes(zstat_slots.at[0 : LAYERS - 1], zstat_sems.at[0])
    wait_bytes(gx.at[0, 0 : CHIPS - 1], gx_sems.at[0])
    wait_bytes(gx.at[0], fwd_sems.at[0])


def body(source_latents, target_latents):
    f32, bf16 = jnp.float32, jnp.bfloat16
    vmem, dma = pltpu.VMEM, pltpu.SemaphoreType.DMA
    row, col = (ROW_TILES, 128), (COL_TILES, 128)
    any_space, in_vmem = pl.BlockSpec(memory_space=pl.ANY), pl.BlockSpec(memory_space=pltpu.VMEM)
    u, v, mass = pl.pallas_call(
        kernel,
        name="sinkhorn",
        out_shape=[jax.ShapeDtypeStruct(shape, f32) for shape in (row, col, row)],
        in_specs=[any_space, any_space],
        out_specs=[in_vmem] * 3,
        scratch_shapes=[
            vmem((WIDTH, WIDTH), f32),
            vmem((128, 128), f32),
            vmem((WIDTH, COLS), f32),
            vmem((COLS, DEPTH), bf16),
            vmem((DEPTH, 256), bf16),
            vmem((COLS, ROWS), f32),
            vmem((2, CHIPS, WIDTH // 2, 128), f32),
            vmem((2, 128), f32),
            vmem((2 * CHIPS, 2, 128), f32),
            vmem((2, 128), f32),
            vmem((LAYERS, 2, 128), f32),
            vmem(row, f32),
            vmem((2,) + row, f32),
            vmem((2, CHIPS) + row, f32),
            vmem(col, f32),
            vmem((2, LAYERS) + col, f32),
            vmem((COLS, 128), f32),
            vmem((COLS, 128), f32),
            vmem(row, f32),
            vmem(row, f32),
            vmem(row, f32),
            vmem(col, f32),
            vmem(col, f32),
            vmem(row, f32),
            dma((2,)),
            dma((2,)),
            dma((2,)),
            dma((2,)),
            dma((2,)),
            dma(()),
            dma((2,)),
            dma(()),
            dma((2,)),
            dma(()),
            dma((2,)),
        ],
        compiler_params=pltpu.CompilerParams(
            collective_id=0, has_side_effects=True, vmem_limit_bytes=40 * 1024 * 1024
        ),
    )(source_latents, target_latents.T)
    return u.reshape(ROWS), v.reshape(COLS), mass.reshape(ROWS)


def solution(mesh):
    in_specs = (P(("src", "tgt"), None), P("tgt", None))
    out_specs = (P("src"), P("tgt"), P("src"))
    return jax.shard_map(body, mesh=mesh, in_specs=in_specs, out_specs=out_specs, check_vma=False)
```

```python
import functools
import math

import jax
import jax.numpy as jnp
from jax import lax
from jax.experimental import pallas as pl
from jax.experimental.pallas import tpu as pltpu
from jax.sharding import PartitionSpec as P

ITERS = 4
EDGE = 4
CHIPS = EDGE * EDGE
LAYERS = 16
WIDTH = 64
ROWS = 2048
COLS = 1024
ROW_TILES = ROWS // 128
COL_TILES = COLS // 128
DEPTH = 8 * WIDTH
CELLS = 32768
LOG_CELLS = math.log2(CELLS)
LIFT = 30.0
SCALE = 90.0
MESH = pl.DeviceIdType.MESH


def hops(step):
    return min(step, EDGE - step)


PLANE = sorted(
    ((dy, dx) for dy in range(EDGE) for dx in range(EDGE) if dy or dx),
    key=lambda step: -hops(step[0]) - hops(step[1]),
)
RING = sorted(range(1, LAYERS), key=lambda step: -min(step, LAYERS - step))


def split3(value):
    high = value.astype(jnp.bfloat16)
    rest = value - high.astype(jnp.float32)
    mid = rest.astype(jnp.bfloat16)
    low = (rest - mid.astype(jnp.float32)).astype(jnp.bfloat16)
    return high, mid, low


def kernel(
    x_hbm, yt_hbm, u_out, v_out,
    x_in, x_pad, yt, ya, xt, tile, powers, gx,
    stat_send, stat_slots, zstat_send, zstat_slots,
    row_send, row_sib, row_slots, col_send, col_slots,
    col_part, col_wide, row_max, row_norm, row_base, row_shift, col_base, col_gain, alpha,
    ring_sem, in_sem, stat_sems, zstat_sems, gx_send_sem, gx_sems, fwd_send_sem, fwd_sems,
    row_send_sem, row_sems, sib_send_sem, sib_sems, col_send_sem, col_sems,
):
    layer = lax.axis_index("src")
    place = lax.axis_index("tgt")
    core = lax.rem(place, 2)
    chip = place // 2
    px = lax.rem(chip, EDGE)
    py = chip // EDGE
    sibling = (layer, chip * 2 + 1 - core)

    def plane_chip(step):
        return lax.rem(py + step[0], EDGE) * EDGE + lax.rem(px + step[1], EDGE)

    plane_same = [(layer, plane_chip(step) * 2 + core) for step in PLANE]
    plane_other = [(layer, plane_chip(step) * 2 + 1 - core) for step in PLANE]
    ring = [(lax.rem(layer + step, LAYERS), place) for step in RING]

    def wait_bytes(ref, sem):
        pltpu.make_async_copy(ref, ref, sem).wait()

    def push(src, dst, send_sem, recv_sem, peer):
        pltpu.make_async_remote_copy(
            src_ref=src, dst_ref=dst, send_sem=send_sem, recv_sem=recv_sem,
            device_id=peer, device_id_type=MESH,
        ).start()

    barrier = pltpu.get_barrier_semaphore()
    near = [(lax.rem(layer + step, LAYERS), place) for step in range(1, LAYERS) if min(step, LAYERS - step) <= LAYERS // 4]
    peers = plane_same + plane_other + [sibling] + near
    for peer in peers:
        pl.semaphore_signal(barrier, inc=1, device_id=peer, device_id_type=MESH)
    x_copy = pltpu.make_async_copy(x_hbm, x_in, in_sem.at[0])
    y_copy = pltpu.make_async_copy(yt_hbm, yt, in_sem.at[1])
    x_copy.start()
    y_copy.start()
    x_pad[...] = jnp.zeros_like(x_pad)
    x_copy.wait()
    x_pad[0:WIDTH, 0:WIDTH] = x_in[...]

    lanes = lax.broadcasted_iota(jnp.int32, (1, 128), 1)
    left = lanes < WIDTH

    x_wide = x_pad[...]
    x_turned = x_wide.T
    gx[core, chip] = x_turned[0:32, :] + pltpu.roll(x_turned[32:64, :], 64, 1)
    x_sum = jnp.sum(x_wide, 0, keepdims=True)
    x_square = jnp.sum(x_wide * x_wide, 0, keepdims=True)

    y_sum = jnp.zeros((1, 128), jnp.float32)
    y_square = jnp.zeros((1, 128), jnp.float32)
    y_copy.wait()
    for block in range(COL_TILES):
        at = slice(block * 128, block * 128 + 128)
        piece = yt[:, at]
        wide = jnp.concatenate([piece, piece], 0).T
        col_wide[at, :] = wide
        y_sum += jnp.sum(wide, 0, keepdims=True)
        y_square += jnp.sum(wide * wide, 0, keepdims=True)
    stat_send[0:1, :] = jnp.where(left, x_sum, y_sum)
    stat_send[1:2, :] = jnp.where(left, x_square, y_square)
    stat_slots[place] = stat_send[...]

    pl.semaphore_wait(barrier, len(peers))
    for step in (LAYERS // 4, LAYERS - LAYERS // 4):
        peer = (lax.rem(layer + step, LAYERS), place)
        pl.semaphore_signal(ring_sem, inc=1, device_id=peer, device_id_type=MESH)

    for peer in plane_same + plane_other + [sibling]:
        push(stat_send, stat_slots.at[place], stat_sems.at[0], stat_sems.at[1], peer)
    for peer in plane_same[::-1]:
        push(gx.at[core, chip], gx.at[core, chip], gx_send_sem, gx_sems.at[chip], peer)

    def forward(at):
        push(gx.at[core, at], gx.at[core, at], fwd_send_sem, fwd_sems.at[at], sibling)

    forward(chip)

    for block in range(COL_TILES):
        at = slice(block * 128, block * 128 + 128)
        wide = col_wide[at, :]
        norm = jnp.sum(jnp.where(left, wide * wide, 0.0), 1, keepdims=True)
        high, mid, low = split3(wide)
        ya[at, 0:128] = high
        ya[at, 128:256] = mid
        ya[at, 256:384] = jnp.where(left, low.astype(jnp.float32), high.astype(jnp.float32)).astype(jnp.bfloat16)
        nh, nm, nl = split3(jnp.broadcast_to(norm, (128, 128)))
        tail = jnp.where(lanes == 0, nh.astype(jnp.float32), jnp.where(lanes == 1, nm.astype(jnp.float32), nl.astype(jnp.float32)))
        ya[at, 384:512] = jnp.where(lanes < 3, tail, 0.0).astype(jnp.bfloat16)
    tail_row = lax.broadcasted_iota(jnp.int32, (128, 256), 0)
    xt[384:512, :] = jnp.where(tail_row < 3, -1.0, 0.0).astype(jnp.bfloat16)

    wait_bytes(stat_slots.at[0 : 2 * CHIPS - 1], stat_sems.at[1])
    zstat_send[...] = jnp.sum(stat_slots[...], 0)
    zstat_slots[layer] = zstat_send[...]
    pl.semaphore_wait(ring_sem, 2)
    for peer in ring:
        push(zstat_send, zstat_slots.at[layer], zstat_sems.at[0], zstat_sems.at[1], peer)

    def pair(step):
        turn = step // 2
        dy = turn + (turn // 2) * (1 - 2 * lax.rem(turn, 2))
        dx = lax.rem(step, 2)
        return lax.rem(py + dy, EDGE) * 2 + lax.rem(px // 2 + dx, 2)

    def receive(at):
        wait_bytes(gx.at[0, 0], gx_sems.at[at])
        forward(at)

    def multiply(q):
        halves = []
        for k in range(2):
            wait_bytes(gx.at[0, 0], fwd_sems.at[2 * q + k])
        for k in range(2):
            one = gx[0, 2 * q + k]
            two = gx[1, 2 * q + k]
            top = jnp.where(left, one, pltpu.roll(two, 64, 1))
            low = jnp.where(left, pltpu.roll(one, 64, 1), two)
            halves.append(jnp.concatenate([top, low], 0))
        full = jnp.concatenate(halves, 1)
        norm = jnp.sum(full * full, 0, keepdims=True)
        high, mid, low = split3(full * 2.0)
        xt[0:64, :] = high
        xt[64:128, :] = mid
        xt[128:192, :] = high
        xt[192:256, :] = mid
        xt[256:320, :] = high
        xt[320:384, :] = low
        product = jnp.dot(ya[...], xt[...], preferred_element_type=jnp.float32)
        tile[:, pl.ds(pl.multiple_of(q * 256, 256), 256)] = product
        top = jnp.max(product, 0, keepdims=True)
        for k in range(2):
            row_max[pl.ds(2 * q + k, 1), :] = top[:, k * 128 : k * 128 + 128]
            row_norm[pl.ds(2 * q + k, 1), :] = norm[:, k * 128 : k * 128 + 128]

    def stage(step, carry):
        ahead = pair(step)
        receive(2 * ahead)
        receive(2 * ahead + 1)
        multiply(pair(step - 1))
        return carry

    receive(chip + 1 - 2 * lax.rem(px, 2))
    lax.fori_loop(1, CHIPS // 2, stage, 0)
    multiply(pair(CHIPS // 2 - 1))

    wait_bytes(zstat_slots.at[0 : LAYERS - 1], zstat_sems.at[1])
    total = jnp.sum(zstat_slots[...], 0) * jnp.where(left, 1.0 / CELLS, 1.0 / (CELLS * LAYERS))
    means = total[0:1, :]
    mean_cost = jnp.sum(total[1:2, :] - means * pltpu.roll(means, 64, 1), 1, keepdims=True)
    kappa = jnp.broadcast_to(math.log2(math.e) / (0.05 * mean_cost), (8, 128))

    def lane(t):
        return slice(t * 128, t * 128 + 128)

    def spread(ref, t):
        return jnp.broadcast_to(ref[t : t + 1, :], (8, 128))

    def row_exchange(parity, join):
        push(row_send, row_sib.at[parity], sib_send_sem, sib_sems.at[parity], sibling)
        wait_bytes(row_sib.at[parity], sib_sems.at[parity])
        wait_bytes(row_send, sib_send_sem)
        both = join(row_send[...], row_sib[parity])
        row_send[...] = both
        row_slots[parity, chip] = both
        for peer in plane_same:
            push(row_send, row_slots.at[parity, chip], row_send_sem, row_sems.at[parity], peer)
        wait_bytes(row_slots.at[parity, 0 : CHIPS - 1], row_sems.at[parity])
        wait_bytes(row_slots.at[parity, 0 : CHIPS - 1], row_send_sem)

    def col_exchange(parity):
        col_slots[parity, layer] = col_send[...]
        for peer in ring:
            push(col_send, col_slots.at[parity, layer], col_send_sem, col_sems.at[parity], peer)
        wait_bytes(col_slots.at[parity, 0 : LAYERS - 1], col_sems.at[parity])
        wait_bytes(col_slots.at[parity, 0 : LAYERS - 1], col_send_sem)

    def lse_pair(a, b):
        top = jnp.maximum(a, b)
        return top + jnp.log2(jnp.exp2(a - top) + jnp.exp2(b - top))

    def lse_slots(slots):
        top = jnp.max(slots, 0)
        return top + jnp.log2(jnp.sum(jnp.exp2(slots - top[None]), 0))

    def col_lanes(ref, pick):
        for block in range(COL_TILES):
            col_send[block : block + 1, :] = pick(ref[block * 128 : block * 128 + 128, :].T)

    def add_sublanes(block):
        return jnp.sum(block, 0, keepdims=True)

    row_max[...] = row_max[...] * kappa[0:1, :]
    GROUP = 8

    tops = [spread(row_max, t) for t in range(ROW_TILES)]

    def first_rows(g, accs):
        accs = list(accs)
        for k in range(GROUP):
            at = pl.ds(pl.multiple_of(g * 8 * GROUP, 8) + 8 * k, 8)
            for t in range(ROW_TILES):
                accs[t] += jnp.exp2(tile[at, lane(t)] * kappa - tops[t])
        return tuple(accs)

    zeros = tuple(jnp.zeros((8, 128), jnp.float32) for _ in range(ROW_TILES))
    accs = lax.fori_loop(0, COLS // (8 * GROUP), first_rows, zeros)
    for t in range(ROW_TILES):
        row_send[t : t + 1, :] = row_max[t : t + 1, :] + jnp.log2(jnp.sum(accs[t], 0, keepdims=True))
    row_exchange(0, lse_pair)
    row_base[...] = -LOG_CELLS - lse_slots(row_slots[0])

    row_shift[...] = row_base[...] / kappa[0:1, :]
    shifts = [spread(row_shift, t) for t in range(ROW_TILES)]

    def tree(parts, join):
        while len(parts) > 1:
            parts = [join(parts[i], parts[i + 1]) for i in range(0, len(parts), 2)]
        return parts[0]

    def first_max(g, carry):
        for k in range(GROUP):
            at = pl.ds(pl.multiple_of(g * 8 * GROUP, 8) + 8 * k, 8)
            col_part[at, :] = tree([tile[at, lane(t)] + shifts[t] for t in range(ROW_TILES)], jnp.maximum)
        return carry

    lax.fori_loop(0, COLS // (8 * GROUP), first_max, 0)
    lift = LIFT / kappa[0:1, :]
    for block in range(COL_TILES):
        at = slice(block * 128, block * 128 + 128)
        col_wide[at, :] = jnp.broadcast_to(jnp.max(col_part[at, :], 1, keepdims=True) - lift, (128, 128))

    def first_cols(g, carry):
        for k in range(GROUP):
            at = pl.ds(pl.multiple_of(g * 8 * GROUP, 8) + 8 * k, 8)
            top = col_wide[at, :]
            parts = []
            for t in range(ROW_TILES):
                power = jnp.exp2((tile[at, lane(t)] + shifts[t] - top) * kappa)
                powers[at, lane(t)] = power
                parts.append(power)
            col_part[at, :] = tree(parts, jnp.add)
        return carry

    lax.fori_loop(0, COLS // (8 * GROUP), first_cols, 0)
    col_lanes(col_wide, lambda block: block[0:1, :])
    col_gain[...] = col_send[...] * kappa
    col_lanes(col_part, add_sublanes)
    col_send[...] = col_gain[...] + jnp.log2(col_send[...])
    col_exchange(0)
    col_base[...] = -LOG_CELLS - lse_slots(col_slots[0])
    col_gain[...] = jnp.exp2(col_gain[...] + col_base[...] + SCALE)

    def spread_cols(value):
        turned = value.T
        for block in range(COL_TILES):
            col_wide[block * 128 : block * 128 + 128, :] = jnp.broadcast_to(turned[:, block : block + 1], (128, 128))

    def row_step(parity):
        def add_rows(g, accs):
            accs = list(accs)
            for k in range(GROUP):
                at = pl.ds(pl.multiple_of(g * 8 * GROUP, 8) + 8 * k, 8)
                gain = col_wide[at, :]
                for t in range(ROW_TILES):
                    accs[t] += powers[at, lane(t)] * gain
            return tuple(accs)

        accs = lax.fori_loop(0, COLS // (8 * GROUP), add_rows, zeros)
        for t in range(ROW_TILES):
            row_send[t : t + 1, :] = jnp.sum(accs[t], 0, keepdims=True)
        row_exchange(parity, jnp.add)
        return jnp.sum(row_slots[parity], 0)

    def col_step(parity):
        alphas = [spread(alpha, t) for t in range(ROW_TILES)]

        def add_cols(g, carry):
            for k in range(GROUP):
                at = pl.ds(pl.multiple_of(g * 8 * GROUP, 8) + 8 * k, 8)
                col_part[at, :] = tree([powers[at, lane(t)] * alphas[t] for t in range(ROW_TILES)], jnp.add)
            return carry

        lax.fori_loop(0, COLS // (8 * GROUP), add_cols, 0)
        col_lanes(col_part, add_sublanes)
        col_send[...] = col_send[...] * col_gain[...]
        col_exchange(parity)
        return jnp.sum(col_slots[parity], 0)

    ratio = 2.0 ** (SCALE - LOG_CELLS)
    spread_cols(col_gain[...])

    def iterate(step, carry):
        parity = lax.rem(step, 2)
        alpha[...] = ratio / row_step(parity)
        beta = ratio / col_step(parity)
        v_out[...] = (col_base[...] + jnp.log2(beta)) * math.log(2.0)
        spread_cols(beta * col_gain[...])
        return carry

    lax.fori_loop(1, ITERS, iterate, 0)
    u_out[0] = alpha[...]
    u_out[1] = row_base[...] + row_norm[...] * kappa[0:1, :]
    u_out[2] = row_step(ITERS % 2) * (1.0 / ratio)
    wait_bytes(stat_slots.at[0 : 2 * CHIPS - 1], stat_sems.at[0])
    wait_bytes(zstat_slots.at[0 : LAYERS - 1], zstat_sems.at[0])
    wait_bytes(gx.at[0, 0 : CHIPS - 1], gx_send_sem)
    wait_bytes(gx.at[0], fwd_send_sem)


def body(source_latents, target_latents):
    f32, bf16 = jnp.float32, jnp.bfloat16
    vmem, dma = pltpu.VMEM, pltpu.SemaphoreType.DMA
    row, col = (ROW_TILES, 128), (COL_TILES, 128)
    in_hbm, in_vmem = pl.BlockSpec(memory_space=pltpu.HBM), pl.BlockSpec(memory_space=pltpu.VMEM)
    rows, v = pl.pallas_call(
        kernel,
        name="sinkhorn",
        out_shape=[jax.ShapeDtypeStruct(shape, f32) for shape in ((3,) + row, col)],
        in_specs=[in_hbm, in_hbm],
        out_specs=[in_vmem] * 2,
        scratch_shapes=[
            vmem((WIDTH, WIDTH), f32),
            vmem((128, 128), f32),
            vmem((WIDTH, COLS), f32),
            vmem((COLS, DEPTH), bf16),
            vmem((DEPTH, 256), bf16),
            vmem((COLS, ROWS), f32),
            vmem((COLS, ROWS), f32),
            vmem((2, CHIPS, WIDTH // 2, 128), f32),
            vmem((2, 128), f32),
            vmem((2 * CHIPS, 2, 128), f32),
            vmem((2, 128), f32),
            vmem((LAYERS, 2, 128), f32),
            vmem(row, f32),
            vmem((2,) + row, f32),
            vmem((2, CHIPS) + row, f32),
            vmem(col, f32),
            vmem((2, LAYERS) + col, f32),
            vmem((COLS, 128), f32),
            vmem((COLS, 128), f32),
            vmem(row, f32),
            vmem(row, f32),
            vmem(row, f32),
            vmem(row, f32),
            vmem(col, f32),
            vmem(col, f32),
            vmem(row, f32),
            pltpu.SemaphoreType.REGULAR,
            dma((2,)),
            dma((2,)),
            dma((2,)),
            dma(()),
            dma((CHIPS,)),
            dma(()),
            dma((CHIPS,)),
            dma(()),
            dma((2,)),
            dma(()),
            dma((2,)),
            dma(()),
            dma((2,)),
        ],
        compiler_params=pltpu.CompilerParams(
            collective_id=0, has_side_effects=True, vmem_limit_bytes=40 * 1024 * 1024
        ),
    )(
        pltpu.with_memory_space_constraint(source_latents, pltpu.HBM),
        pltpu.with_memory_space_constraint(target_latents.T, pltpu.HBM),
    )
    factor, first, mass = rows[0], rows[1], rows[2]
    u = (first + jnp.log2(factor)) * math.log(2.0)
    return u.reshape(ROWS), v.reshape(COLS), (factor * mass).reshape(ROWS)


def solution(mesh):
    in_specs = (P(("src", "tgt"), None), P("tgt", None))
    out_specs = (P("src"), P("tgt"), P("src"))
    return jax.shard_map(body, mesh=mesh, in_specs=in_specs, out_specs=out_specs, check_vma=False)
```

```python
import functools
import math

import jax
import jax.numpy as jnp
from jax import lax
from jax.experimental import pallas as pl
from jax.experimental.pallas import tpu as pltpu
from jax.sharding import PartitionSpec as P

ITERS = 4
EDGE = 4
CHIPS = EDGE * EDGE
LAYERS = 16
WIDTH = 64
ROWS = 2048
COLS = 1024
ROW_TILES = ROWS // 128
COL_TILES = COLS // 128
DEPTH = 8 * WIDTH
CELLS = 32768
LOG_CELLS = math.log2(CELLS)
LIFT = 30.0
SCALE = 90.0
FAR_HOPS = 9
MESH = pl.DeviceIdType.MESH


def hops(step):
    return min(step, EDGE - step)


PLANE = sorted(
    ((dy, dx) for dy in range(EDGE) for dx in range(EDGE) if dy or dx),
    key=lambda step: -hops(step[0]) - hops(step[1]),
)
FAR = [step for step in PLANE if hops(step[0]) + hops(step[1]) >= FAR_HOPS]
RING = sorted(range(1, LAYERS), key=lambda step: -min(step, LAYERS - step))


def split3(value):
    high = value.astype(jnp.bfloat16)
    rest = value - high.astype(jnp.float32)
    mid = rest.astype(jnp.bfloat16)
    low = (rest - mid.astype(jnp.float32)).astype(jnp.bfloat16)
    return high, mid, low


def kernel(
    x_hbm, yt_hbm, u_out, v_out,
    x_in, x_pad, yt, ya, xt, tile, powers, gx,
    stat_send, stat_slots, zstat_send, zstat_slots,
    row_send, row_both, row_sib, row_slots, col_send, col_slots,
    col_part, col_wide, row_max, row_norm, row_base, row_shift, col_base, col_gain, alpha, beta,
    ring_sem, in_sem, stat_sems, zstat_sems, gx_send_sem, gx_sems, fwd_send_sem, fwd_sems,
    row_send_sem, row_sems, sib_send_sem, sib_sems, col_send_sem, col_sems,
):
    layer = lax.axis_index("src")
    place = lax.axis_index("tgt")
    core = lax.rem(place, 2)
    chip = place // 2
    px = lax.rem(chip, EDGE)
    py = chip // EDGE
    sibling = (layer, chip * 2 + 1 - core)

    def plane_chip(step):
        return lax.rem(py + step[0], EDGE) * EDGE + lax.rem(px + step[1], EDGE)

    plane_same = [(layer, plane_chip(step) * 2 + core) for step in PLANE]
    plane_other = [(layer, plane_chip(step) * 2 + 1 - core) for step in PLANE]
    plane_both = [peer for both in zip(plane_same, plane_other) for peer in both] + [sibling]
    ring = [(lax.rem(layer + step, LAYERS), place) for step in RING]

    def wait_bytes(ref, sem):
        pltpu.make_async_copy(ref, ref, sem).wait()

    def push(src, dst, send_sem, recv_sem, peer):
        pltpu.make_async_remote_copy(
            src_ref=src, dst_ref=dst, send_sem=send_sem, recv_sem=recv_sem,
            device_id=peer, device_id_type=MESH,
        ).start()

    x_copy = pltpu.make_async_copy(x_hbm, x_in, in_sem.at[0])
    y_copy = pltpu.make_async_copy(yt_hbm, yt, in_sem.at[1])
    x_copy.start()
    y_copy.start()
    barrier = pltpu.get_barrier_semaphore()
    near = [(lax.rem(layer + step, LAYERS), place) for step in RING if min(step, LAYERS - step) <= LAYERS // 4]
    peers = near[:2] + plane_both + near[2:]
    for peer in peers:
        pl.semaphore_signal(barrier, inc=1, device_id=peer, device_id_type=MESH)
    x_pad[...] = jnp.zeros_like(x_pad)
    x_copy.wait()
    x_pad[0:WIDTH, 0:WIDTH] = x_in[...]

    lanes = lax.broadcasted_iota(jnp.int32, (1, 128), 1)
    left = lanes < WIDTH

    x_wide = x_pad[...]
    x_turned = x_wide.T
    gx[core, chip] = x_turned[0:32, :] + pltpu.roll(x_turned[32:64, :], 64, 1)
    x_sum = jnp.sum(x_wide, 0, keepdims=True)
    x_square = jnp.sum(x_wide * x_wide, 0, keepdims=True)

    y_sum = jnp.zeros((1, 128), jnp.float32)
    y_square = jnp.zeros((1, 128), jnp.float32)
    y_copy.wait()
    for block in range(COL_TILES):
        at = slice(block * 128, block * 128 + 128)
        piece = yt[:, at]
        wide = jnp.concatenate([piece, piece], 0).T
        col_wide[at, :] = wide
        y_sum += jnp.sum(wide, 0, keepdims=True)
        y_square += jnp.sum(wide * wide, 0, keepdims=True)
    stat_send[0:1, :] = jnp.where(left, x_sum, y_sum)
    stat_send[1:2, :] = jnp.where(left, x_square, y_square)
    stat_slots[place] = stat_send[...]

    pl.semaphore_wait(barrier, len(peers))
    for step in (LAYERS // 4, LAYERS - LAYERS // 4):
        peer = (lax.rem(layer + step, LAYERS), place)
        pl.semaphore_signal(ring_sem, inc=1, device_id=peer, device_id_type=MESH)

    for peer in plane_both:
        push(stat_send, stat_slots.at[place], stat_sems.at[0], stat_sems.at[1], peer)
    for peer in plane_same[::-1]:
        push(gx.at[core, chip], gx.at[core, chip], gx_send_sem, gx_sems.at[chip], peer)

    def forward(at):
        push(gx.at[core, at], gx.at[core, at], fwd_send_sem, fwd_sems.at[at], sibling)

    forward(chip)

    for block in range(COL_TILES):
        at = slice(block * 128, block * 128 + 128)
        wide = col_wide[at, :]
        norm = jnp.sum(jnp.where(left, wide * wide, 0.0), 1, keepdims=True)
        high, mid, low = split3(wide)
        ya[at, 0:128] = high
        ya[at, 128:256] = mid
        ya[at, 256:384] = jnp.where(left, low.astype(jnp.float32), high.astype(jnp.float32)).astype(jnp.bfloat16)
        nh, nm, nl = split3(jnp.broadcast_to(norm, (128, 128)))
        tail = jnp.where(lanes == 0, nh.astype(jnp.float32), jnp.where(lanes == 1, nm.astype(jnp.float32), nl.astype(jnp.float32)))
        ya[at, 384:512] = jnp.where(lanes < 3, tail, 0.0).astype(jnp.bfloat16)
    tail_row = lax.broadcasted_iota(jnp.int32, (128, 256), 0)
    xt[384:512, :] = jnp.where(tail_row < 3, -1.0, 0.0).astype(jnp.bfloat16)

    wait_bytes(stat_slots.at[0 : 2 * CHIPS - 1], stat_sems.at[1])
    zstat_send[...] = jnp.sum(stat_slots[...], 0)
    zstat_slots[layer] = zstat_send[...]
    pl.semaphore_wait(ring_sem, 2)
    for peer in ring:
        push(zstat_send, zstat_slots.at[layer], zstat_sems.at[0], zstat_sems.at[1], peer)

    def pair(step):
        turn = step // 2
        dy = turn + (turn // 2) * (1 - 2 * lax.rem(turn, 2))
        dx = lax.rem(step, 2)
        return lax.rem(py + dy, EDGE) * 2 + lax.rem(px // 2 + dx, 2)

    def receive(at):
        wait_bytes(gx.at[0, 0], gx_sems.at[at])
        forward(at)

    def multiply(q):
        halves = []
        for k in range(2):
            wait_bytes(gx.at[0, 0], fwd_sems.at[2 * q + k])
        for k in range(2):
            one = gx[0, 2 * q + k]
            two = gx[1, 2 * q + k]
            top = jnp.where(left, one, pltpu.roll(two, 64, 1))
            low = jnp.where(left, pltpu.roll(one, 64, 1), two)
            halves.append(jnp.concatenate([top, low], 0))
        full = jnp.concatenate(halves, 1)
        norm = jnp.sum(full * full, 0, keepdims=True)
        high, mid, low = split3(full * 2.0)
        xt[0:64, :] = high
        xt[64:128, :] = mid
        xt[128:192, :] = high
        xt[192:256, :] = mid
        xt[256:320, :] = high
        xt[320:384, :] = low
        product = jnp.dot(ya[...], xt[...], preferred_element_type=jnp.float32)
        tile[:, pl.ds(pl.multiple_of(q * 256, 256), 256)] = product
        top = jnp.max(product, 0, keepdims=True)
        for k in range(2):
            row_max[pl.ds(2 * q + k, 1), :] = top[:, k * 128 : k * 128 + 128]
            row_norm[pl.ds(2 * q + k, 1), :] = norm[:, k * 128 : k * 128 + 128]

    def stage(step, carry):
        ahead = pair(step)
        receive(2 * ahead)
        receive(2 * ahead + 1)
        multiply(pair(step - 1))
        return carry

    receive(chip + 1 - 2 * lax.rem(px, 2))
    lax.fori_loop(1, CHIPS // 2, stage, 0)
    multiply(pair(CHIPS // 2 - 1))

    wait_bytes(zstat_slots.at[0 : LAYERS - 1], zstat_sems.at[1])
    total = jnp.sum(zstat_slots[...], 0) * jnp.where(left, 1.0 / CELLS, 1.0 / (CELLS * LAYERS))
    means = total[0:1, :]
    mean_cost = jnp.sum(total[1:2, :] - means * pltpu.roll(means, 64, 1), 1, keepdims=True)
    kappa = jnp.broadcast_to(math.log2(math.e) / (0.05 * mean_cost), (8, 128))

    def lane(t):
        return slice(t * 128, t * 128 + 128)

    def spread(ref, t):
        return jnp.broadcast_to(ref[t : t + 1, :], (8, 128))

    def row_exchange(parity, join):
        arrived = row_sems.at[parity]
        push(row_send, row_sib.at[parity], sib_send_sem, sib_sems.at[parity], sibling)
        for step, same, other in zip(PLANE, plane_same, plane_other):
            if step in FAR:
                back = FAR.index(((EDGE - step[0]) % EDGE, (EDGE - step[1]) % EDGE))
                push(row_send, row_slots.at[parity, chip], row_send_sem, arrived, same)
                push(row_send, row_slots.at[parity, CHIPS + back], row_send_sem, arrived, other)
        wait_bytes(row_sib.at[parity], sib_sems.at[parity])
        row_both[...] = join(row_send[...], row_sib[parity])
        for step, same in zip(PLANE, plane_same):
            if step not in FAR:
                push(row_both, row_slots.at[parity, chip], row_send_sem, arrived, same)
        row_slots[parity, chip] = row_both[...]
        wait_bytes(row_slots.at[parity, 0 : CHIPS - 1 + len(FAR)], arrived)
        for k, step in enumerate(FAR):
            at = plane_chip(step)
            row_slots[parity, at] = join(row_slots[parity, at], row_slots[parity, CHIPS + k])
        wait_bytes(row_send, sib_send_sem)
        wait_bytes(row_slots.at[parity, 0 : CHIPS - 1 + len(FAR)], row_send_sem)

    def col_exchange(parity):
        col_slots[parity, layer] = col_send[...]
        for peer in ring:
            push(col_send, col_slots.at[parity, layer], col_send_sem, col_sems.at[parity], peer)
        wait_bytes(col_slots.at[parity, 0 : LAYERS - 1], col_sems.at[parity])
        wait_bytes(col_slots.at[parity, 0 : LAYERS - 1], col_send_sem)

    def lse_pair(a, b):
        top = jnp.maximum(a, b)
        return top + jnp.log2(jnp.exp2(a - top) + jnp.exp2(b - top))

    def lse_slots(slots):
        top = jnp.max(slots, 0)
        return top + jnp.log2(jnp.sum(jnp.exp2(slots - top[None]), 0))

    def col_lanes(ref, pick):
        for block in range(COL_TILES):
            col_send[block : block + 1, :] = pick(ref[block * 128 : block * 128 + 128, :].T)

    def add_sublanes(block):
        return jnp.sum(block, 0, keepdims=True)

    row_max[...] = row_max[...] * kappa[0:1, :]
    GROUP = 16

    tops = [spread(row_max, t) for t in range(ROW_TILES)]

    def first_rows(g, accs):
        accs = list(accs)
        for k in range(GROUP):
            at = pl.ds(pl.multiple_of(g * 8 * GROUP, 8) + 8 * k, 8)
            for t in range(ROW_TILES):
                accs[t] += jnp.exp2(tile[at, lane(t)] * kappa - tops[t])
        return tuple(accs)

    zeros = tuple(jnp.zeros((8, 128), jnp.float32) for _ in range(ROW_TILES))
    accs = lax.fori_loop(0, COLS // (8 * GROUP), first_rows, zeros)
    for t in range(ROW_TILES):
        row_send[t : t + 1, :] = row_max[t : t + 1, :] + jnp.log2(jnp.sum(accs[t], 0, keepdims=True))
    row_exchange(0, lse_pair)
    row_base[...] = -LOG_CELLS - lse_slots(row_slots[0, 0:CHIPS])

    row_shift[...] = row_base[...] / kappa[0:1, :]
    shifts = [spread(row_shift, t) for t in range(ROW_TILES)]

    def tree(parts, join):
        while len(parts) > 1:
            parts = [join(parts[i], parts[i + 1]) for i in range(0, len(parts), 2)]
        return parts[0]

    def first_max(g, carry):
        for k in range(GROUP):
            at = pl.ds(pl.multiple_of(g * 8 * GROUP, 8) + 8 * k, 8)
            col_part[at, :] = tree([tile[at, lane(t)] + shifts[t] for t in range(ROW_TILES)], jnp.maximum)
        return carry

    lax.fori_loop(0, COLS // (8 * GROUP), first_max, 0)
    lift = LIFT / kappa[0:1, :]
    for block in range(COL_TILES):
        at = slice(block * 128, block * 128 + 128)
        col_wide[at, :] = jnp.broadcast_to(jnp.max(col_part[at, :], 1, keepdims=True) - lift, (128, 128))

    def first_cols(g, carry):
        for k in range(GROUP):
            at = pl.ds(pl.multiple_of(g * 8 * GROUP, 8) + 8 * k, 8)
            top = col_wide[at, :]
            parts = []
            for t in range(ROW_TILES):
                power = jnp.exp2((tile[at, lane(t)] + shifts[t] - top) * kappa)
                powers[at, lane(t)] = power
                parts.append(power)
            col_part[at, :] = tree(parts, jnp.add)
        return carry

    lax.fori_loop(0, COLS // (8 * GROUP), first_cols, 0)
    col_lanes(col_wide, lambda block: block[0:1, :])
    col_gain[...] = col_send[...] * kappa
    col_lanes(col_part, add_sublanes)
    col_send[...] = col_gain[...] + jnp.log2(col_send[...])
    col_exchange(0)
    col_base[...] = -LOG_CELLS - lse_slots(col_slots[0])
    col_gain[...] = jnp.exp2(col_gain[...] + col_base[...] + SCALE)

    def row_step(parity, gains):
        turned = gains.T
        accs = list(zeros)
        for block in range(COL_TILES):
            for k in range(16):
                gain = jnp.broadcast_to(turned[8 * k : 8 * k + 8, block : block + 1], (8, 128))
                at = slice(128 * block + 8 * k, 128 * block + 8 * k + 8)
                for t in range(ROW_TILES):
                    accs[t] += powers[at, lane(t)] * gain
        for t in range(ROW_TILES):
            row_send[t : t + 1, :] = jnp.sum(accs[t], 0, keepdims=True)
        row_exchange(parity, jnp.add)
        return jnp.sum(row_slots[parity, 0:CHIPS], 0)

    def col_step(parity):
        alphas = [spread(alpha, t) for t in range(ROW_TILES)]
        for block in range(COL_TILES):
            parts = []
            for k in range(16):
                at = slice(128 * block + 8 * k, 128 * block + 8 * k + 8)
                parts.append(tree([powers[at, lane(t)] * alphas[t] for t in range(ROW_TILES)], jnp.add))
            total = jnp.sum(jnp.concatenate(parts, 0).T, 0, keepdims=True)
            col_send[block : block + 1, :] = total * col_gain[block : block + 1, :]
        col_exchange(parity)
        return jnp.sum(col_slots[parity], 0)

    ratio = 2.0 ** (SCALE - LOG_CELLS)

    def iterate(step, gains):
        parity = lax.rem(step, 2)
        alpha[...] = ratio / row_step(parity, gains)
        beta[...] = ratio / col_step(parity)
        return beta[...] * col_gain[...]

    u_out[1] = row_base[...] + row_norm[...] * kappa[0:1, :]
    gains = lax.fori_loop(1, ITERS, iterate, col_gain[...])
    u_out[0] = alpha[...]
    v_out[...] = (col_base[...] + jnp.log2(beta[...])) * math.log(2.0)
    u_out[2] = row_step(ITERS % 2, gains) * (1.0 / ratio)
    wait_bytes(stat_slots.at[0 : 2 * CHIPS - 1], stat_sems.at[0])
    wait_bytes(zstat_slots.at[0 : LAYERS - 1], zstat_sems.at[0])
    wait_bytes(gx.at[0, 0 : CHIPS - 1], gx_send_sem)
    wait_bytes(gx.at[0], fwd_send_sem)


def body(source_latents, target_latents):
    f32, bf16 = jnp.float32, jnp.bfloat16
    vmem, dma = pltpu.VMEM, pltpu.SemaphoreType.DMA
    row, col = (ROW_TILES, 128), (COL_TILES, 128)
    in_hbm, in_vmem = pl.BlockSpec(memory_space=pltpu.HBM), pl.BlockSpec(memory_space=pltpu.VMEM)
    rows, v = pl.pallas_call(
        kernel,
        name="sinkhorn",
        out_shape=[jax.ShapeDtypeStruct(shape, f32) for shape in ((3,) + row, col)],
        in_specs=[in_hbm, in_hbm],
        out_specs=[in_vmem] * 2,
        scratch_shapes=[
            vmem((WIDTH, WIDTH), f32),
            vmem((128, 128), f32),
            vmem((WIDTH, COLS), f32),
            vmem((COLS, DEPTH), bf16),
            vmem((DEPTH, 256), bf16),
            vmem((COLS, ROWS), f32),
            vmem((COLS, ROWS), f32),
            vmem((2, CHIPS, WIDTH // 2, 128), f32),
            vmem((2, 128), f32),
            vmem((2 * CHIPS, 2, 128), f32),
            vmem((2, 128), f32),
            vmem((LAYERS, 2, 128), f32),
            vmem(row, f32),
            vmem(row, f32),
            vmem((2,) + row, f32),
            vmem((2, CHIPS + len(FAR)) + row, f32),
            vmem(col, f32),
            vmem((2, LAYERS) + col, f32),
            vmem((COLS, 128), f32),
            vmem((COLS, 128), f32),
            vmem(row, f32),
            vmem(row, f32),
            vmem(row, f32),
            vmem(row, f32),
            vmem(col, f32),
            vmem(col, f32),
            vmem(row, f32),
            vmem(col, f32),
            pltpu.SemaphoreType.REGULAR,
            dma((2,)),
            dma((2,)),
            dma((2,)),
            dma(()),
            dma((CHIPS,)),
            dma(()),
            dma((CHIPS,)),
            dma(()),
            dma((2,)),
            dma(()),
            dma((2,)),
            dma(()),
            dma((2,)),
        ],
        compiler_params=pltpu.CompilerParams(
            collective_id=0, has_side_effects=True, vmem_limit_bytes=40 * 1024 * 1024
        ),
    )(
        pltpu.with_memory_space_constraint(source_latents, pltpu.HBM),
        pltpu.with_memory_space_constraint(target_latents.T, pltpu.HBM),
    )
    factor, first, mass = rows[0], rows[1], rows[2]
    u = (first + jnp.log2(factor)) * math.log(2.0)
    return u.reshape(ROWS), v.reshape(COLS), (factor * mass).reshape(ROWS)


def solution(mesh):
    in_specs = (P(("src", "tgt"), None), P("tgt", None))
    out_specs = (P("src"), P("tgt"), P("src"))
    return jax.shard_map(body, mesh=mesh, in_specs=in_specs, out_specs=out_specs, check_vma=False)
```

```python
import functools
import math

import jax
import jax.numpy as jnp
from jax import lax
from jax.experimental import pallas as pl
from jax.experimental.pallas import tpu as pltpu
from jax.sharding import PartitionSpec as P

ITERS = 4
EDGE = 4
CHIPS = EDGE * EDGE
LAYERS = 16
WIDTH = 64
ROWS = 2048
COLS = 1024
ROW_TILES = ROWS // 128
COL_TILES = COLS // 128
DEPTH = 8 * WIDTH
CELLS = 32768
LOG_CELLS = math.log2(CELLS)
LIFT = 30.0
SCALE = 90.0
FAR_HOPS = 4
MESH = pl.DeviceIdType.MESH


def hops(step):
    return min(step, EDGE - step)


PLANE = sorted(
    ((dy, dx) for dy in range(EDGE) for dx in range(EDGE) if dy or dx),
    key=lambda step: -hops(step[0]) - hops(step[1]),
)
FAR = [step for step in PLANE if hops(step[0]) + hops(step[1]) >= FAR_HOPS]
RING = sorted(range(1, LAYERS), key=lambda step: -min(step, LAYERS - step))


def split3(value):
    high = value.astype(jnp.bfloat16)
    rest = value - high.astype(jnp.float32)
    mid = rest.astype(jnp.bfloat16)
    low = (rest - mid.astype(jnp.float32)).astype(jnp.bfloat16)
    return high, mid, low


def kernel(
    x_hbm, yt_hbm, u_out, v_out,
    x_in, x_pad, yt, ya, xt, tile, powers, gx,
    stat_send, stat_slots, zstat_send, zstat_slots,
    row_send, row_both, row_sib, row_slots, col_send, col_slots,
    col_part, col_wide, row_max, row_norm, row_base, row_shift, col_base, col_gain, alpha, beta,
    ring_sem, in_sem, stat_sems, zstat_sems, gx_send_sem, gx_sems, fwd_send_sem, fwd_sems,
    row_send_sem, row_sems, sib_send_sem, sib_sems, col_send_sem, col_sems,
):
    layer = lax.axis_index("src")
    place = lax.axis_index("tgt")
    core = lax.rem(place, 2)
    chip = place // 2
    px = lax.rem(chip, EDGE)
    py = chip // EDGE
    sibling = (layer, chip * 2 + 1 - core)

    def plane_chip(step):
        return lax.rem(py + step[0], EDGE) * EDGE + lax.rem(px + step[1], EDGE)

    plane_same = [(layer, plane_chip(step) * 2 + core) for step in PLANE]
    plane_other = [(layer, plane_chip(step) * 2 + 1 - core) for step in PLANE]
    plane_both = [peer for both in zip(plane_same, plane_other) for peer in both] + [sibling]
    ring = [(lax.rem(layer + step, LAYERS), place) for step in RING]

    def wait_bytes(ref, sem):
        pltpu.make_async_copy(ref, ref, sem).wait()

    def push(src, dst, send_sem, recv_sem, peer):
        pltpu.make_async_remote_copy(
            src_ref=src, dst_ref=dst, send_sem=send_sem, recv_sem=recv_sem,
            device_id=peer, device_id_type=MESH,
        ).start()

    x_copy = pltpu.make_async_copy(x_hbm, x_in, in_sem.at[0])
    y_copy = pltpu.make_async_copy(yt_hbm, yt, in_sem.at[1])
    x_copy.start()
    y_copy.start()
    barrier = pltpu.get_barrier_semaphore()
    near = [(lax.rem(layer + step, LAYERS), place) for step in RING if min(step, LAYERS - step) <= LAYERS // 4]
    peers = near[:2] + plane_both + near[2:]
    for peer in peers:
        pl.semaphore_signal(barrier, inc=1, device_id=peer, device_id_type=MESH)
    x_pad[...] = jnp.zeros_like(x_pad)
    x_copy.wait()
    x_pad[0:WIDTH, 0:WIDTH] = x_in[...]

    lanes = lax.broadcasted_iota(jnp.int32, (1, 128), 1)
    left = lanes < WIDTH

    x_wide = x_pad[...]
    x_turned = x_wide.T
    gx[core, chip] = x_turned[0:32, :] + pltpu.roll(x_turned[32:64, :], 64, 1)
    x_sum = jnp.sum(x_wide, 0, keepdims=True)
    x_square = jnp.sum(x_wide * x_wide, 0, keepdims=True)

    y_sum = jnp.zeros((1, 128), jnp.float32)
    y_square = jnp.zeros((1, 128), jnp.float32)
    y_copy.wait()
    for block in range(COL_TILES):
        at = slice(block * 128, block * 128 + 128)
        piece = yt[:, at]
        wide = jnp.concatenate([piece, piece], 0).T
        col_wide[at, :] = wide
        y_sum += jnp.sum(wide, 0, keepdims=True)
        y_square += jnp.sum(wide * wide, 0, keepdims=True)
    stat_send[0:1, :] = jnp.where(left, x_sum, y_sum)
    stat_send[1:2, :] = jnp.where(left, x_square, y_square)
    stat_slots[place] = stat_send[...]

    pl.semaphore_wait(barrier, len(peers))
    for step in (LAYERS // 4, LAYERS - LAYERS // 4):
        peer = (lax.rem(layer + step, LAYERS), place)
        pl.semaphore_signal(ring_sem, inc=1, device_id=peer, device_id_type=MESH)

    for peer in plane_both:
        push(stat_send, stat_slots.at[place], stat_sems.at[0], stat_sems.at[1], peer)
    for peer in plane_same[::-1]:
        push(gx.at[core, chip], gx.at[core, chip], gx_send_sem, gx_sems.at[chip], peer)

    def forward(at):
        push(gx.at[core, at], gx.at[core, at], fwd_send_sem, fwd_sems.at[at], sibling)

    forward(chip)

    for block in range(COL_TILES):
        at = slice(block * 128, block * 128 + 128)
        wide = col_wide[at, :]
        norm = jnp.sum(jnp.where(left, wide * wide, 0.0), 1, keepdims=True)
        high, mid, low = split3(wide)
        ya[at, 0:128] = high
        ya[at, 128:256] = mid
        ya[at, 256:384] = jnp.where(left, low.astype(jnp.float32), high.astype(jnp.float32)).astype(jnp.bfloat16)
        nh, nm, nl = split3(jnp.broadcast_to(norm, (128, 128)))
        tail = jnp.where(lanes == 0, nh.astype(jnp.float32), jnp.where(lanes == 1, nm.astype(jnp.float32), nl.astype(jnp.float32)))
        ya[at, 384:512] = jnp.where(lanes < 3, tail, 0.0).astype(jnp.bfloat16)
    tail_row = lax.broadcasted_iota(jnp.int32, (128, 256), 0)
    xt[384:512, :] = jnp.where(tail_row < 3, -1.0, 0.0).astype(jnp.bfloat16)

    wait_bytes(stat_slots.at[0 : 2 * CHIPS - 1], stat_sems.at[1])
    zstat_send[...] = jnp.sum(stat_slots[...], 0)
    zstat_slots[layer] = zstat_send[...]
    pl.semaphore_wait(ring_sem, 2)
    for peer in ring:
        push(zstat_send, zstat_slots.at[layer], zstat_sems.at[0], zstat_sems.at[1], peer)

    def pair(step):
        turn = step // 2
        dy = turn + (turn // 2) * (1 - 2 * lax.rem(turn, 2))
        dx = lax.rem(step, 2)
        return lax.rem(py + dy, EDGE) * 2 + lax.rem(px // 2 + dx, 2)

    def receive(at):
        wait_bytes(gx.at[0, 0], gx_sems.at[at])
        forward(at)

    def multiply(q):
        halves = []
        for k in range(2):
            wait_bytes(gx.at[0, 0], fwd_sems.at[2 * q + k])
        for k in range(2):
            one = gx[0, 2 * q + k]
            two = gx[1, 2 * q + k]
            top = jnp.where(left, one, pltpu.roll(two, 64, 1))
            low = jnp.where(left, pltpu.roll(one, 64, 1), two)
            halves.append(jnp.concatenate([top, low], 0))
        full = jnp.concatenate(halves, 1)
        norm = jnp.sum(full * full, 0, keepdims=True)
        high, mid, low = split3(full * 2.0)
        xt[0:64, :] = high
        xt[64:128, :] = mid
        xt[128:192, :] = high
        xt[192:256, :] = mid
        xt[256:320, :] = high
        xt[320:384, :] = low
        product = jnp.dot(ya[...], xt[...], preferred_element_type=jnp.float32)
        tile[:, pl.ds(pl.multiple_of(q * 256, 256), 256)] = product
        top = jnp.max(product, 0, keepdims=True)
        for k in range(2):
            row_max[pl.ds(2 * q + k, 1), :] = top[:, k * 128 : k * 128 + 128]
            row_norm[pl.ds(2 * q + k, 1), :] = norm[:, k * 128 : k * 128 + 128]

    def stage(step, carry):
        ahead = pair(step)
        receive(2 * ahead)
        receive(2 * ahead + 1)
        multiply(pair(step - 1))
        return carry

    receive(chip + 1 - 2 * lax.rem(px, 2))
    lax.fori_loop(1, CHIPS // 2, stage, 0)
    multiply(pair(CHIPS // 2 - 1))

    wait_bytes(zstat_slots.at[0 : LAYERS - 1], zstat_sems.at[1])
    total = jnp.sum(zstat_slots[...], 0) * jnp.where(left, 1.0 / CELLS, 1.0 / (CELLS * LAYERS))
    means = total[0:1, :]
    mean_cost = jnp.sum(total[1:2, :] - means * pltpu.roll(means, 64, 1), 1, keepdims=True)
    kappa = jnp.broadcast_to(math.log2(math.e) / (0.05 * mean_cost), (8, 128))

    def lane(t):
        return slice(t * 128, t * 128 + 128)

    def spread(ref, t):
        return jnp.broadcast_to(ref[t : t + 1, :], (8, 128))

    def row_exchange(parity, join):
        arrived = row_sems.at[parity]
        push(row_send, row_sib.at[parity], sib_send_sem, sib_sems.at[parity], sibling)
        for step, same, other in zip(PLANE, plane_same, plane_other):
            if step in FAR:
                back = FAR.index(((EDGE - step[0]) % EDGE, (EDGE - step[1]) % EDGE))
                push(row_send, row_slots.at[parity, chip], row_send_sem, arrived, same)
                push(row_send, row_slots.at[parity, CHIPS + back], row_send_sem, arrived, other)
        wait_bytes(row_sib.at[parity], sib_sems.at[parity])
        row_both[...] = join(row_send[...], row_sib[parity])
        for step, same in zip(PLANE, plane_same):
            if step not in FAR:
                push(row_both, row_slots.at[parity, chip], row_send_sem, arrived, same)
        row_slots[parity, chip] = row_both[...]
        wait_bytes(row_slots.at[parity, 0 : CHIPS - 1 + len(FAR)], arrived)
        for k, step in enumerate(FAR):
            at = plane_chip(step)
            row_slots[parity, at] = join(row_slots[parity, at], row_slots[parity, CHIPS + k])
        wait_bytes(row_send, sib_send_sem)
        wait_bytes(row_slots.at[parity, 0 : CHIPS - 1 + len(FAR)], row_send_sem)

    def col_exchange(parity):
        col_slots[parity, layer] = col_send[...]
        for peer in ring:
            push(col_send, col_slots.at[parity, layer], col_send_sem, col_sems.at[parity], peer)
        wait_bytes(col_slots.at[parity, 0 : LAYERS - 1], col_sems.at[parity])
        wait_bytes(col_slots.at[parity, 0 : LAYERS - 1], col_send_sem)

    def lse_pair(a, b):
        top = jnp.maximum(a, b)
        return top + jnp.log2(jnp.exp2(a - top) + jnp.exp2(b - top))

    def lse_slots(slots):
        top = jnp.max(slots, 0)
        return top + jnp.log2(jnp.sum(jnp.exp2(slots - top[None]), 0))

    def col_lanes(ref, pick):
        for block in range(COL_TILES):
            col_send[block : block + 1, :] = pick(ref[block * 128 : block * 128 + 128, :].T)

    def add_sublanes(block):
        return jnp.sum(block, 0, keepdims=True)

    row_max[...] = row_max[...] * kappa[0:1, :]
    GROUP = 32

    tops = [spread(row_max, t) for t in range(ROW_TILES)]

    def first_rows(g, accs):
        accs = list(accs)
        for k in range(GROUP):
            at = pl.ds(pl.multiple_of(g * 8 * GROUP, 8) + 8 * k, 8)
            for t in range(ROW_TILES):
                accs[t] += jnp.exp2(tile[at, lane(t)] * kappa - tops[t])
        return tuple(accs)

    zeros = tuple(jnp.zeros((8, 128), jnp.float32) for _ in range(ROW_TILES))
    accs = lax.fori_loop(0, COLS // (8 * GROUP), first_rows, zeros)
    for t in range(ROW_TILES):
        row_send[t : t + 1, :] = row_max[t : t + 1, :] + jnp.log2(jnp.sum(accs[t], 0, keepdims=True))
    row_exchange(0, lse_pair)
    row_base[...] = -LOG_CELLS - lse_slots(row_slots[0, 0:CHIPS])

    row_shift[...] = row_base[...] / kappa[0:1, :]
    shifts = [spread(row_shift, t) for t in range(ROW_TILES)]

    def tree(parts, join):
        while len(parts) > 1:
            parts = [join(parts[i], parts[i + 1]) for i in range(0, len(parts), 2)]
        return parts[0]

    def first_max(g, carry):
        for k in range(GROUP):
            at = pl.ds(pl.multiple_of(g * 8 * GROUP, 8) + 8 * k, 8)
            col_part[at, :] = tree([tile[at, lane(t)] + shifts[t] for t in range(ROW_TILES)], jnp.maximum)
        return carry

    lax.fori_loop(0, COLS // (8 * GROUP), first_max, 0)
    lift = LIFT / kappa[0:1, :]
    for block in range(COL_TILES):
        at = slice(block * 128, block * 128 + 128)
        col_wide[at, :] = jnp.broadcast_to(jnp.max(col_part[at, :], 1, keepdims=True) - lift, (128, 128))

    def first_cols(g, carry):
        for k in range(GROUP):
            at = pl.ds(pl.multiple_of(g * 8 * GROUP, 8) + 8 * k, 8)
            top = col_wide[at, :]
            parts = []
            for t in range(ROW_TILES):
                power = jnp.exp2((tile[at, lane(t)] + shifts[t] - top) * kappa)
                powers[at, lane(t)] = power
                parts.append(power)
            col_part[at, :] = tree(parts, jnp.add)
        return carry

    lax.fori_loop(0, COLS // (8 * GROUP), first_cols, 0)
    col_lanes(col_wide, lambda block: block[0:1, :])
    col_gain[...] = col_send[...] * kappa
    col_lanes(col_part, add_sublanes)
    col_send[...] = col_gain[...] + jnp.log2(col_send[...])
    col_exchange(0)
    col_base[...] = -LOG_CELLS - lse_slots(col_slots[0])
    col_gain[...] = jnp.exp2(col_gain[...] + col_base[...] + SCALE)

    def row_step(parity, gains):
        turned = gains.T
        accs = list(zeros)
        for block in range(COL_TILES):
            for k in range(16):
                gain = jnp.broadcast_to(turned[8 * k : 8 * k + 8, block : block + 1], (8, 128))
                at = slice(128 * block + 8 * k, 128 * block + 8 * k + 8)
                for t in range(ROW_TILES):
                    accs[t] += powers[at, lane(t)] * gain
        for t in range(ROW_TILES):
            row_send[t : t + 1, :] = jnp.sum(accs[t], 0, keepdims=True)
        row_exchange(parity, jnp.add)
        return jnp.sum(row_slots[parity, 0:CHIPS], 0)

    def col_step(parity):
        alphas = [spread(alpha, t) for t in range(ROW_TILES)]
        for block in range(COL_TILES):
            parts = []
            for k in range(16):
                at = slice(128 * block + 8 * k, 128 * block + 8 * k + 8)
                parts.append(tree([powers[at, lane(t)] * alphas[t] for t in range(ROW_TILES)], jnp.add))
            total = jnp.sum(jnp.concatenate(parts, 0).T, 0, keepdims=True)
            col_send[block : block + 1, :] = total * col_gain[block : block + 1, :]
        col_exchange(parity)
        return jnp.sum(col_slots[parity], 0)

    ratio = 2.0 ** (SCALE - LOG_CELLS)

    def iterate(step, gains):
        parity = lax.rem(step, 2)
        alpha[...] = ratio / row_step(parity, gains)
        beta[...] = ratio / col_step(parity)
        return beta[...] * col_gain[...]

    u_out[1] = row_base[...] + row_norm[...] * kappa[0:1, :]
    gains = lax.fori_loop(1, ITERS, iterate, col_gain[...])
    u_out[0] = alpha[...]
    v_out[...] = (col_base[...] + jnp.log2(beta[...])) * math.log(2.0)
    u_out[2] = row_step(ITERS % 2, gains) * (1.0 / ratio)
    wait_bytes(stat_slots.at[0 : 2 * CHIPS - 1], stat_sems.at[0])
    wait_bytes(zstat_slots.at[0 : LAYERS - 1], zstat_sems.at[0])
    wait_bytes(gx.at[0, 0 : CHIPS - 1], gx_send_sem)
    wait_bytes(gx.at[0], fwd_send_sem)


def body(source_latents, target_latents):
    f32, bf16 = jnp.float32, jnp.bfloat16
    vmem, dma = pltpu.VMEM, pltpu.SemaphoreType.DMA
    row, col = (ROW_TILES, 128), (COL_TILES, 128)
    in_hbm, in_vmem = pl.BlockSpec(memory_space=pltpu.HBM), pl.BlockSpec(memory_space=pltpu.VMEM)
    rows, v = pl.pallas_call(
        kernel,
        name="sinkhorn",
        out_shape=[jax.ShapeDtypeStruct(shape, f32) for shape in ((3,) + row, col)],
        in_specs=[in_hbm, in_hbm],
        out_specs=[in_vmem] * 2,
        scratch_shapes=[
            vmem((WIDTH, WIDTH), f32),
            vmem((128, 128), f32),
            vmem((WIDTH, COLS), f32),
            vmem((COLS, DEPTH), bf16),
            vmem((DEPTH, 256), bf16),
            vmem((COLS, ROWS), f32),
            vmem((COLS, ROWS), f32),
            vmem((2, CHIPS, WIDTH // 2, 128), f32),
            vmem((2, 128), f32),
            vmem((2 * CHIPS, 2, 128), f32),
            vmem((2, 128), f32),
            vmem((LAYERS, 2, 128), f32),
            vmem(row, f32),
            vmem(row, f32),
            vmem((2,) + row, f32),
            vmem((2, CHIPS + len(FAR)) + row, f32),
            vmem(col, f32),
            vmem((2, LAYERS) + col, f32),
            vmem((COLS, 128), f32),
            vmem((COLS, 128), f32),
            vmem(row, f32),
            vmem(row, f32),
            vmem(row, f32),
            vmem(row, f32),
            vmem(col, f32),
            vmem(col, f32),
            vmem(row, f32),
            vmem(col, f32),
            pltpu.SemaphoreType.REGULAR,
            dma((2,)),
            dma((2,)),
            dma((2,)),
            dma(()),
            dma((CHIPS,)),
            dma(()),
            dma((CHIPS,)),
            dma(()),
            dma((2,)),
            dma(()),
            dma((2,)),
            dma(()),
            dma((2,)),
        ],
        compiler_params=pltpu.CompilerParams(
            collective_id=0, has_side_effects=True, vmem_limit_bytes=40 * 1024 * 1024
        ),
    )(
        pltpu.with_memory_space_constraint(source_latents, pltpu.HBM),
        pltpu.with_memory_space_constraint(target_latents.T, pltpu.HBM),
    )
    factor, first, mass = rows[0], rows[1], rows[2]
    u = (first + jnp.log2(factor)) * math.log(2.0)
    return u.reshape(ROWS), v.reshape(COLS), (factor * mass).reshape(ROWS)


def solution(mesh):
    in_specs = (P(("src", "tgt"), None), P("tgt", None))
    out_specs = (P("src"), P("tgt"), P("src"))
    return jax.shard_map(body, mesh=mesh, in_specs=in_specs, out_specs=out_specs, check_vma=False)
```
